32 devices in a mesh: grp: 2 (over y), blk: 16 (over z, x, core).
Axes of the slice: x: 2, y: 2, z: 4, core: 2. Of those that a mesh axis runs over, the one named last changes fastest.
Arguments:
- amplitudes: bfloat16 [32, 640, 640], P('grp', 'blk'), parts along dimension 0, may hold values from -0.009765625 to 0.009765625
- factors: bfloat16 [16, 640, 2560], P('blk'), may hold values from -0.875 to 0.875
Outputs:
- residual: float32 [16, 3, 32], P('blk', None, 'grp'), parts along dimension 2
The draws below stay inside these ranges and needn't reach their ends.
There are 2 independent parts, one for each index of `grp`. The reference program is written for one: setup_inputs(seed, part) draws one part's arguments, and reference() takes and returns one part's arrays. A program takes and returns all parts, laid end to end along the dimension named above; an argument that names none is the same for every part. Nothing has to cross between parts.
All inputs are finite; a program needn't handle non-finite values.
Results may differ from the reference program's by a relative error of at most 0.003.
Values may be sent and summed in bfloat16 or wider, within the bound.
A program may use at most 64 MiB of HBM per device.

```python
import jax
import jax.numpy as jnp
from jax import lax

NV = 640
NAUX = 2560
NP = 16
NW = 16


def levels(key, shape, shards, low, top_value):
    gain, own = 1.0, jax.random.fold_in(key, 6)
    for axis_at, shards_of in shards:
        heights = jnp.exp(jax.random.uniform(jax.random.fold_in(own, axis_at), (shards_of,), jnp.float32, low / len(shards), top_value / len(shards)))
        gain = gain * jnp.repeat(heights, shape[axis_at] // shards_of).reshape([-1 if axis == axis_at else 1 for axis in range(len(shape))])
    return gain


def noise(rng, shape, deviation, reach, cuts=(), held_as=jnp.bfloat16):
    array = deviation * jax.random.normal(rng, shape, jnp.float32)
    if cuts:
        array = array * levels(rng, shape, cuts, -0.22, 0.18)
    return jnp.clip(array, -reach, reach).astype(held_as)


def setup_inputs(seed: int = 0, part: int = 0) -> dict:
    keys = jax.random.split(jax.random.key(seed), 3)
    part_keys = jax.random.split(jax.random.fold_in(keys[2], part), 3)
    return {
        "amplitudes": noise(part_keys[0], (NP, NV, NV), (NV * NV) ** -0.5, 0.009765625, ((1, 16),)),
        "factors": noise(keys[1], (NW, NV, NAUX), 0.14, 0.875, ((0, 16),)),
    }


def reference(amplitudes, factors):
    amps_wide = amplitudes.astype(jnp.float32)

    def one_window(index):
        first = factors[index]
        second = factors[(index + 1) % NW]
        v_aa = jnp.dot(first, first.T, preferred_element_type=jnp.float32).astype(jnp.bfloat16)
        v_ab = jnp.dot(first, second.T, preferred_element_type=jnp.float32).astype(jnp.bfloat16)
        v_ba = jnp.dot(second, first.T, preferred_element_type=jnp.float32).astype(jnp.bfloat16)
        terms = [jnp.einsum("pcd,cd->p", amps_wide, tile.astype(jnp.float32)) for tile in (v_aa, v_ab, v_ba)]
        return jnp.stack(terms, axis=0)

    return lax.map(one_window, jnp.arange(NW, dtype=jnp.int32))
```

```python
import functools

import jax
import jax.numpy as jnp
from jax import lax
from jax.experimental import pallas as pl
from jax.experimental.pallas import tpu as pltpu
from jax.sharding import PartitionSpec as P

MESH = pl.DeviceIdType.MESH
CHUNKS = 4
NT = (((1,), (1,)), ((), ()))


def kernel(
    n,
    t_hbm,
    f_hbm,
    out_ref,
    own,
    near,
    amps,
    cast_off,
    both,
    made,
    got,
    part,
    back,
    local_sem,
    near_send,
    near_recv,
    relay_send,
    amp_sem,
    made_send,
    got_recv,
    part_send,
    back_recv,
):
    g = lax.axis_index("grp")
    m = lax.axis_index("blk")
    other = 1 - g
    behind = lax.rem(m + n - 1, n)
    odd = lax.rem(m, 2)
    pairs, rows, wide = t_hbm.shape
    half = wide // 2
    span = half // CHUNKS

    copy_f = pltpu.make_async_copy(f_hbm, own, local_sem.at[0])
    copy_t = pltpu.make_async_copy(t_hbm, amps, local_sem.at[1])
    copy_f.start()
    copy_t.start()

    barrier = pltpu.get_barrier_semaphore()

    @pl.loop(1, n)
    def _(s):
        pl.semaphore_signal(barrier, inc=1, device_id=(g, lax.rem(m + s, n)), device_id_type=MESH)

    @pl.loop(0, n)
    def _(s):
        pl.semaphore_signal(barrier, inc=1, device_id=(other, lax.rem(m + s, n)), device_id_type=MESH)

    pl.semaphore_wait(barrier, 2 * n - 1)

    def near_copy(h, q):
        return pltpu.make_async_remote_copy(
            src_ref=f_hbm.at[h, pl.ds(q * span, span)],
            dst_ref=near.at[h, pl.ds(q * span, span)],
            send_sem=near_send.at[h, q],
            recv_sem=near_recv.at[h, q],
            device_id=(g, behind),
            device_id_type=MESH,
        )

    def relay_copy(q):
        return pltpu.make_async_remote_copy(
            src_ref=near.at[g, pl.ds(q * span, span)],
            dst_ref=near.at[g, pl.ds(q * span, span)],
            send_sem=relay_send.at[q],
            recv_sem=near_recv.at[g, q],
            device_id=(other, m),
            device_id_type=MESH,
        )

    for q in range(CHUNKS):
        near_copy(g, q).start()

    @pl.when(odd == 1)
    def _():
        for q in range(CHUNKS):
            near_copy(other, q).start()

    copy_t.wait()
    left = amps[:, :, :half]
    right = amps[:, :, half:]
    low = g == 0
    both[g] = jnp.where(low, left, right)
    cast_off[...] = jnp.where(low, right, left)
    amp_copy = pltpu.make_async_remote_copy(
        src_ref=cast_off,
        dst_ref=both.at[g],
        send_sem=amp_sem.at[0],
        recv_sem=amp_sem.at[1],
        device_id=(other, m),
        device_id_type=MESH,
    )
    amp_copy.start()

    blocks = n // 2

    def product(k, left_ref, h, right_ref):
        tile = lax.dot_general(
            left_ref[h], right_ref[g], NT, preferred_element_type=jnp.float32
        )
        for b in range(blocks):
            made[k, h * blocks + b] = tile[b * rows : (b + 1) * rows].astype(jnp.bfloat16)

    def made_copy(k, s):
        to = lax.rem(m + n - s, n)
        return pltpu.make_async_remote_copy(
            src_ref=made.at[k, to],
            dst_ref=got.at[k, s],
            send_sem=made_send.at[k, s],
            recv_sem=got_recv.at[k, s],
            device_id=(g, to),
            device_id_type=MESH,
        )

    def send(k):
        @pl.loop(1, n)
        def _(s):
            made_copy(k, s).start()

        got[k, 0] = made[k, m]

    copy_f.wait()
    for h in range(2):
        product(0, own, h, own)
    send(0)

    for q in range(CHUNKS):
        near_copy(g, q).wait_recv()

        @pl.when(odd == 1)
        def _():
            relay_copy(q).start()

    for h in range(2):
        product(1, own, h, near)
    send(1)
    product(2, near, g, own)
    for q in range(CHUNKS):
        near_copy(other, q).wait_recv()
    product(2, near, other, own)
    send(2)

    amp_copy.wait_recv()
    flat = both[...].astype(jnp.float32).reshape(2 * pairs * rows, half).astype(jnp.bfloat16)
    columns = 2 * pairs * rows
    on_diagonal = lax.broadcasted_iota(jnp.int32, (rows, columns), 0) == lax.rem(
        lax.broadcasted_iota(jnp.int32, (rows, columns), 1), rows
    )
    lane = lax.broadcasted_iota(jnp.int32, (columns, 128), 0)
    first = lax.broadcasted_iota(jnp.int32, (columns, 128), 1) * rows
    chooser = jnp.where((lane >= first) & (lane < first + rows), 1.0, 0.0)
    part[...] = jnp.zeros_like(part)
    for k in range(3):

        @pl.loop(1, n)
        def _(s):
            made_copy(k, s).wait_recv()

        tiles = got[k].astype(jnp.float32).reshape(n * rows, half).astype(jnp.bfloat16)
        grid = lax.dot_general(tiles, flat, NT, preferred_element_type=jnp.float32)
        grid = jnp.where(on_diagonal[None], grid.reshape(n, rows, columns), 0.0)
        sums = jnp.dot(
            jnp.sum(grid, axis=1),
            chooser,
            preferred_element_type=jnp.float32,
            precision=lax.Precision.HIGHEST,
        )
        for s in range(n):
            part[s, k : k + 1] = sums[s : s + 1]

    def part_copy(plane, s):
        return pltpu.make_async_remote_copy(
            src_ref=part.at[s],
            dst_ref=back.at[g, s],
            send_sem=part_send.at[plane, s],
            recv_sem=back_recv.at[g, s],
            device_id=(plane, lax.rem(m + s, n)),
            device_id_type=MESH,
        )

    def back_wait(plane, s):
        return pltpu.make_async_remote_copy(
            src_ref=part.at[s],
            dst_ref=back.at[plane, s],
            send_sem=part_send.at[plane, s],
            recv_sem=back_recv.at[plane, s],
            device_id=(plane, lax.rem(m + n - s, n)),
            device_id_type=MESH,
        )

    @pl.loop(0, n)
    def _(s):
        part_copy(other, s).start()

    @pl.loop(1, n)
    def _(s):
        part_copy(g, s).start()

    back[g, 0] = part[0]

    @pl.loop(1, n)
    def _(s):
        back_wait(g, s).wait_recv()

    @pl.loop(0, n)
    def _(s):
        back_wait(other, s).wait_recv()

    total = jnp.sum(back[...].reshape(2 * n, 8, 128), axis=0)
    out_ref[0] = jnp.where(low, total[:3, :pairs], total[:3, pairs : 2 * pairs])

    for q in range(CHUNKS):
        near_copy(g, q).wait_send()

    @pl.when(odd == 1)
    def _():
        for q in range(CHUNKS):
            near_copy(other, q).wait_send()
            relay_copy(q).wait_send()

    amp_copy.wait_send()
    for k in range(3):

        @pl.loop(1, n)
        def _(s):
            made_copy(k, s).wait_send()

    @pl.loop(0, n)
    def _(s):
        part_copy(other, s).wait_send()

    @pl.loop(1, n)
    def _(s):
        part_copy(g, s).wait_send()


def fused(n, amplitudes, factors):
    pairs, rows, wide = amplitudes.shape
    deep = factors.shape[2]
    half = wide // 2
    dma = pltpu.SemaphoreType.DMA
    bf16 = jnp.bfloat16
    return pl.pallas_call(
        functools.partial(kernel, n),
        out_shape=jax.ShapeDtypeStruct((1, 3, pairs), jnp.float32),
        in_specs=[pl.BlockSpec(memory_space=pl.ANY)] * 2,
        out_specs=pl.BlockSpec(memory_space=pltpu.VMEM),
        scratch_shapes=[
            pltpu.VMEM((2, half, deep), bf16),
            pltpu.VMEM((2, half, deep), bf16),
            pltpu.VMEM((pairs, rows, wide), bf16),
            pltpu.VMEM((pairs, rows, half), bf16),
            pltpu.VMEM((2, pairs, rows, half), bf16),
            pltpu.VMEM((3, n, rows, half), bf16),
            pltpu.VMEM((3, n, rows, half), bf16),
            pltpu.VMEM((n, 8, 128), jnp.float32),
            pltpu.VMEM((2, n, 8, 128), jnp.float32),
            dma((2,)),
            dma((2, CHUNKS)),
            dma((2, CHUNKS)),
            dma((CHUNKS,)),
            dma((2,)),
            dma((3, n)),
            dma((3, n)),
            dma((2, n)),
            dma((2, n)),
        ],
        compiler_params=pltpu.CompilerParams(
            collective_id=0, has_side_effects=True, vmem_limit_bytes=48 * 2**20
        ),
    )(amplitudes, factors.reshape(2, half, deep))


def product_rows(left, right):
    return lax.dot_general(left, right, NT, preferred_element_type=jnp.float32).astype(jnp.bfloat16)


def gathered(n, amplitudes, factors):
    own = factors[0]
    near = lax.ppermute(factors, "blk", [(i, (i + n - 1) % n) for i in range(n)])[0]
    block = lax.all_gather(amplitudes, "blk", axis=1, tiled=True)
    cross = product_rows(own, near)
    tiles = jnp.stack([product_rows(own, own), cross, cross.T])
    total = jnp.einsum("pcd,kcd->kp", block, tiles, preferred_element_type=jnp.float32)
    return total[None]


def solution(mesh):
    n = mesh.shape["blk"]

    def body(amplitudes, factors):
        whole = amplitudes.shape[1] % 8 == 0 and n % 2 == 0 and mesh.shape["grp"] == 2
        return (fused if whole else gathered)(n, amplitudes, factors)

    return jax.shard_map(
        body,
        mesh=mesh,
        in_specs=(P("grp", "blk", None), P("blk", None, None)),
        out_specs=P("blk", None, "grp"),
        check_vma=False,
    )
```

```python
import functools

import jax
import jax.numpy as jnp
from jax import lax
from jax.experimental import pallas as pl
from jax.experimental.pallas import tpu as pltpu
from jax.sharding import PartitionSpec as P

MESH = pl.DeviceIdType.MESH
CHUNKS = 2
NT = (((1,), (1,)), ((), ()))


def kernel(
    n,
    t_hbm,
    f_hbm,
    out_ref,
    own,
    near,
    amps,
    cast_off,
    both,
    made,
    got,
    part,
    back,
    local_sem,
    near_send,
    near_recv,
    relay_send,
    amp_sem,
    made_send,
    got_recv,
    part_send,
    back_recv,
):
    g = lax.axis_index("grp")
    m = lax.axis_index("blk")
    other = 1 - g
    behind = lax.rem(m + n - 1, n)
    odd = lax.rem(m, 2)
    pairs, rows, wide = t_hbm.shape
    half = wide // 2
    span = half // CHUNKS

    copy_f = pltpu.make_async_copy(f_hbm, own, local_sem.at[0])
    copy_t = pltpu.make_async_copy(t_hbm, amps, local_sem.at[1])
    copy_f.start()
    copy_t.start()

    barrier = pltpu.get_barrier_semaphore()

    @pl.loop(1, n)
    def _(s):
        pl.semaphore_signal(barrier, inc=1, device_id=(g, lax.rem(m + s, n)), device_id_type=MESH)

    @pl.loop(0, n)
    def _(s):
        pl.semaphore_signal(barrier, inc=1, device_id=(other, lax.rem(m + s, n)), device_id_type=MESH)

    pl.semaphore_wait(barrier, 2 * n - 1)

    def near_copy(h, q):
        return pltpu.make_async_remote_copy(
            src_ref=f_hbm.at[h, pl.ds(q * span, span)],
            dst_ref=near.at[h, pl.ds(q * span, span)],
            send_sem=near_send.at[h, q],
            recv_sem=near_recv.at[h, q],
            device_id=(g, behind),
            device_id_type=MESH,
        )

    def relay_copy(q):
        return pltpu.make_async_remote_copy(
            src_ref=near.at[g, pl.ds(q * span, span)],
            dst_ref=near.at[g, pl.ds(q * span, span)],
            send_sem=relay_send.at[q],
            recv_sem=near_recv.at[g, q],
            device_id=(other, m),
            device_id_type=MESH,
        )

    for q in range(CHUNKS):
        near_copy(g, q).start()

    @pl.when(odd == 1)
    def _():
        for q in range(CHUNKS):
            near_copy(other, q).start()

    copy_t.wait()
    left = amps[:, :, :half]
    right = amps[:, :, half:]
    low = g == 0
    both[g] = jnp.where(low, left, right)
    cast_off[...] = jnp.where(low, right, left)
    amp_copy = pltpu.make_async_remote_copy(
        src_ref=cast_off,
        dst_ref=both.at[g],
        send_sem=amp_sem.at[0],
        recv_sem=amp_sem.at[1],
        device_id=(other, m),
        device_id_type=MESH,
    )
    amp_copy.start()

    blocks = n // 2

    def product(k, left_ref, h, right_ref):
        tile = lax.dot_general(
            left_ref[h], right_ref[g], NT, preferred_element_type=jnp.float32
        )
        for b in range(blocks):
            made[k, h * blocks + b] = tile[b * rows : (b + 1) * rows].astype(jnp.bfloat16)

    def made_copy(k, s):
        to = lax.rem(m + n - s, n)
        return pltpu.make_async_remote_copy(
            src_ref=made.at[k, to],
            dst_ref=got.at[k, s],
            send_sem=made_send.at[k, s],
            recv_sem=got_recv.at[k, s],
            device_id=(g, to),
            device_id_type=MESH,
        )

    def send(k):
        @pl.loop(1, n)
        def _(s):
            made_copy(k, s).start()

        got[k, 0] = made[k, m]

    copy_f.wait()
    for h in range(2):
        product(0, own, h, own)
    send(0)

    for q in range(CHUNKS):
        near_copy(g, q).wait_recv()

        @pl.when(odd == 1)
        def _():
            relay_copy(q).start()

    for h in range(2):
        product(1, own, h, near)
    send(1)
    product(2, near, g, own)
    for q in range(CHUNKS):
        near_copy(other, q).wait_recv()
    product(2, near, other, own)
    send(2)

    amp_copy.wait_recv()
    flat = both[...].astype(jnp.float32).reshape(2 * pairs * rows, half).astype(jnp.bfloat16)
    columns = 2 * pairs * rows
    on_diagonal = lax.broadcasted_iota(jnp.int32, (rows, columns), 0) == lax.rem(
        lax.broadcasted_iota(jnp.int32, (rows, columns), 1), rows
    )
    lane = lax.broadcasted_iota(jnp.int32, (columns, 128), 0)
    first = lax.broadcasted_iota(jnp.int32, (columns, 128), 1) * rows
    chooser = jnp.where((lane >= first) & (lane < first + rows), 1.0, 0.0)
    part[...] = jnp.zeros_like(part)
    for k in range(3):

        @pl.loop(1, n)
        def _(s):
            made_copy(k, s).wait_recv()

        tiles = got[k].astype(jnp.float32).reshape(n * rows, half).astype(jnp.bfloat16)
        grid = lax.dot_general(tiles, flat, NT, preferred_element_type=jnp.float32)
        grid = jnp.where(on_diagonal[None], grid.reshape(n, rows, columns), 0.0)
        sums = jnp.dot(
            jnp.sum(grid, axis=1),
            chooser,
            preferred_element_type=jnp.float32,
            precision=lax.Precision.HIGHEST,
        )
        for s in range(n):
            part[s, k : k + 1] = sums[s : s + 1]

    def part_copy(plane, s):
        return pltpu.make_async_remote_copy(
            src_ref=part.at[s],
            dst_ref=back.at[g, s],
            send_sem=part_send.at[plane, s],
            recv_sem=back_recv.at[g, s],
            device_id=(plane, lax.rem(m + s, n)),
            device_id_type=MESH,
        )

    def back_wait(plane, s):
        return pltpu.make_async_remote_copy(
            src_ref=part.at[s],
            dst_ref=back.at[plane, s],
            send_sem=part_send.at[plane, s],
            recv_sem=back_recv.at[plane, s],
            device_id=(plane, lax.rem(m + n - s, n)),
            device_id_type=MESH,
        )

    @pl.loop(0, n)
    def _(s):
        part_copy(other, s).start()

    @pl.loop(1, n)
    def _(s):
        part_copy(g, s).start()

    back[g, 0] = part[0]

    @pl.loop(1, n)
    def _(s):
        back_wait(g, s).wait_recv()

    @pl.loop(0, n)
    def _(s):
        back_wait(other, s).wait_recv()

    total = jnp.sum(back[...].reshape(2 * n, 8, 128), axis=0)
    out_ref[0] = jnp.where(low, total[:3, :pairs], total[:3, pairs : 2 * pairs])

    for q in range(CHUNKS):
        near_copy(g, q).wait_send()

    @pl.when(odd == 1)
    def _():
        for q in range(CHUNKS):
            near_copy(other, q).wait_send()
            relay_copy(q).wait_send()

    amp_copy.wait_send()
    for k in range(3):

        @pl.loop(1, n)
        def _(s):
            made_copy(k, s).wait_send()

    @pl.loop(0, n)
    def _(s):
        part_copy(other, s).wait_send()

    @pl.loop(1, n)
    def _(s):
        part_copy(g, s).wait_send()


def fused(n, amplitudes, factors):
    pairs, rows, wide = amplitudes.shape
    deep = factors.shape[2]
    half = wide // 2
    dma = pltpu.SemaphoreType.DMA
    bf16 = jnp.bfloat16
    return pl.pallas_call(
        functools.partial(kernel, n),
        out_shape=jax.ShapeDtypeStruct((1, 3, pairs), jnp.float32),
        in_specs=[pl.BlockSpec(memory_space=pl.ANY)] * 2,
        out_specs=pl.BlockSpec(memory_space=pltpu.VMEM),
        scratch_shapes=[
            pltpu.VMEM((2, half, deep), bf16),
            pltpu.VMEM((2, half, deep), bf16),
            pltpu.VMEM((pairs, rows, wide), bf16),
            pltpu.VMEM((pairs, rows, half), bf16),
            pltpu.VMEM((2, pairs, rows, half), bf16),
            pltpu.VMEM((3, n, rows, half), bf16),
            pltpu.VMEM((3, n, rows, half), bf16),
            pltpu.VMEM((n, 8, 128), jnp.float32),
            pltpu.VMEM((2, n, 8, 128), jnp.float32),
            dma((2,)),
            dma((2, CHUNKS)),
            dma((2, CHUNKS)),
            dma((CHUNKS,)),
            dma((2,)),
            dma((3, n)),
            dma((3, n)),
            dma((2, n)),
            dma((2, n)),
        ],
        compiler_params=pltpu.CompilerParams(
            collective_id=0, has_side_effects=True, vmem_limit_bytes=61 * 2**20
        ),
    )(amplitudes, factors.reshape(2, half, deep))


def product_rows(left, right):
    return lax.dot_general(left, right, NT, preferred_element_type=jnp.float32).astype(jnp.bfloat16)


def gathered(n, amplitudes, factors):
    own = factors[0]
    near = lax.ppermute(factors, "blk", [(i, (i + n - 1) % n) for i in range(n)])[0]
    block = lax.all_gather(amplitudes, "blk", axis=1, tiled=True)
    cross = product_rows(own, near)
    tiles = jnp.stack([product_rows(own, own), cross, cross.T])
    total = jnp.einsum("pcd,kcd->kp", block, tiles, preferred_element_type=jnp.float32)
    return total[None]


def solution(mesh):
    n = mesh.shape["blk"]

    def body(amplitudes, factors):
        whole = amplitudes.shape[1] % 8 == 0 and n % 2 == 0 and mesh.shape["grp"] == 2
        return (fused if whole else gathered)(n, amplitudes, factors)

    return jax.shard_map(
        body,
        mesh=mesh,
        in_specs=(P("grp", "blk", None), P("blk", None, None)),
        out_specs=P("blk", None, "grp"),
        check_vma=False,
    )
```

```python
import functools

import jax
import jax.numpy as jnp
from jax import lax
from jax.experimental import pallas as pl
from jax.experimental.pallas import tpu as pltpu
from jax.sharding import PartitionSpec as P

MESH = pl.DeviceIdType.MESH
CHUNKS = 2
NT = (((1,), (1,)), ((), ()))


def kernel(
    n,
    t_hbm,
    f_hbm,
    out_ref,
    own,
    near,
    amps,
    cast_off,
    both,
    made,
    got,
    part,
    back,
    local_sem,
    near_send,
    near_recv,
    relay_send,
    amp_sem,
    made_send,
    got_recv,
    part_send,
    back_recv,
):
    g = lax.axis_index("grp")
    m = lax.axis_index("blk")
    other = 1 - g
    behind = lax.rem(m + n - 1, n)
    odd = lax.rem(m, 2)
    pairs, rows, wide = t_hbm.shape
    half = wide // 2
    span = half // CHUNKS

    copy_f = pltpu.make_async_copy(f_hbm, own, local_sem.at[0])
    copy_t = pltpu.make_async_copy(t_hbm, amps, local_sem.at[1])
    copy_f.start()
    copy_t.start()

    barrier = pltpu.get_barrier_semaphore()

    @pl.loop(1, n)
    def _(s):
        pl.semaphore_signal(barrier, inc=1, device_id=(g, lax.rem(m + s, n)), device_id_type=MESH)

    @pl.loop(0, n)
    def _(s):
        pl.semaphore_signal(barrier, inc=1, device_id=(other, lax.rem(m + s, n)), device_id_type=MESH)

    copy_t.wait()
    left = amps[:, :, :half]
    right = amps[:, :, half:]
    low = g == 0
    both[g] = jnp.where(low, left, right)
    cast_off[...] = jnp.where(low, right, left)

    blocks = n // 2

    def product(k, left_ref, h, right_ref):
        tile = lax.dot_general(
            left_ref[h], right_ref[g], NT, preferred_element_type=jnp.float32
        )
        for b in range(blocks):
            made[k, h * blocks + b] = tile[b * rows : (b + 1) * rows].astype(jnp.bfloat16)

    copy_f.wait()
    for h in range(2):
        product(0, own, h, own)

    pl.semaphore_wait(barrier, 2 * n - 1)

    def near_copy(h, q):
        return pltpu.make_async_remote_copy(
            src_ref=f_hbm.at[h, pl.ds(q * span, span)],
            dst_ref=near.at[h, pl.ds(q * span, span)],
            send_sem=near_send.at[h, q],
            recv_sem=near_recv.at[h, q],
            device_id=(g, behind),
            device_id_type=MESH,
        )

    def relay_copy(q):
        return pltpu.make_async_remote_copy(
            src_ref=near.at[g, pl.ds(q * span, span)],
            dst_ref=near.at[g, pl.ds(q * span, span)],
            send_sem=relay_send.at[q],
            recv_sem=near_recv.at[g, q],
            device_id=(other, m),
            device_id_type=MESH,
        )

    for q in range(CHUNKS):
        near_copy(g, q).start()

    @pl.when(odd == 1)
    def _():
        for q in range(CHUNKS):
            near_copy(other, q).start()

    amp_copy = pltpu.make_async_remote_copy(
        src_ref=cast_off,
        dst_ref=both.at[g],
        send_sem=amp_sem.at[0],
        recv_sem=amp_sem.at[1],
        device_id=(other, m),
        device_id_type=MESH,
    )
    amp_copy.start()

    def made_copy(k, s):
        to = lax.rem(m + n - s, n)
        return pltpu.make_async_remote_copy(
            src_ref=made.at[k, to],
            dst_ref=got.at[k, s],
            send_sem=made_send.at[k, s],
            recv_sem=got_recv.at[k, s],
            device_id=(g, to),
            device_id_type=MESH,
        )

    def send(k):
        @pl.loop(1, n)
        def _(s):
            made_copy(k, s).start()

        got[k, 0] = made[k, m]

    send(0)

    for q in range(CHUNKS):
        near_copy(g, q).wait_recv()

        @pl.when(odd == 1)
        def _():
            relay_copy(q).start()

    for h in range(2):
        product(1, own, h, near)
    for q in range(CHUNKS):
        near_copy(g, q).wait_send()
    send(1)
    product(2, near, g, own)
    for q in range(CHUNKS):
        near_copy(other, q).wait_recv()
    product(2, near, other, own)
    send(2)

    amp_copy.wait_recv()
    flat = both[...].astype(jnp.float32).reshape(2 * pairs * rows, half).astype(jnp.bfloat16)
    columns = 2 * pairs * rows
    on_diagonal = lax.broadcasted_iota(jnp.int32, (rows, columns), 0) == lax.rem(
        lax.broadcasted_iota(jnp.int32, (rows, columns), 1), rows
    )
    lane = lax.broadcasted_iota(jnp.int32, (columns, 128), 0)
    first = lax.broadcasted_iota(jnp.int32, (columns, 128), 1) * rows
    chooser = jnp.where((lane >= first) & (lane < first + rows), 1.0, 0.0)
    part[...] = jnp.zeros_like(part)
    for k in range(3):

        @pl.loop(1, n)
        def _(s):
            made_copy(k, s).wait_recv()

        tiles = got[k].astype(jnp.float32).reshape(n * rows, half).astype(jnp.bfloat16)
        grid = lax.dot_general(tiles, flat, NT, preferred_element_type=jnp.float32)
        grid = jnp.where(on_diagonal[None], grid.reshape(n, rows, columns), 0.0)
        sums = jnp.dot(
            jnp.sum(grid, axis=1),
            chooser,
            preferred_element_type=jnp.float32,
            precision=lax.Precision.HIGHEST,
        )
        for s in range(n):
            part[s, k : k + 1] = sums[s : s + 1]

    def part_copy(plane, s):
        return pltpu.make_async_remote_copy(
            src_ref=part.at[s],
            dst_ref=back.at[g, s],
            send_sem=part_send.at[plane, s],
            recv_sem=back_recv.at[g, s],
            device_id=(plane, lax.rem(m + s, n)),
            device_id_type=MESH,
        )

    def back_wait(plane, s):
        return pltpu.make_async_remote_copy(
            src_ref=part.at[s],
            dst_ref=back.at[plane, s],
            send_sem=part_send.at[plane, s],
            recv_sem=back_recv.at[plane, s],
            device_id=(plane, lax.rem(m + n - s, n)),
            device_id_type=MESH,
        )

    @pl.loop(0, n)
    def _(s):
        part_copy(other, s).start()

    @pl.loop(1, n)
    def _(s):
        part_copy(g, s).start()

    back[g, 0] = part[0]

    @pl.loop(1, n)
    def _(s):
        back_wait(g, s).wait_recv()

    @pl.loop(0, n)
    def _(s):
        back_wait(other, s).wait_recv()

    total = jnp.sum(back[...].reshape(2 * n, 8, 128), axis=0)
    out_ref[0] = jnp.where(low, total[:3, :pairs], total[:3, pairs : 2 * pairs])

    @pl.when(odd == 1)
    def _():
        for q in range(CHUNKS):
            near_copy(other, q).wait_send()
            relay_copy(q).wait_send()

    amp_copy.wait_send()
    for k in range(3):

        @pl.loop(1, n)
        def _(s):
            made_copy(k, s).wait_send()

    @pl.loop(0, n)
    def _(s):
        part_copy(other, s).wait_send()

    @pl.loop(1, n)
    def _(s):
        part_copy(g, s).wait_send()


def fused(n, amplitudes, factors):
    pairs, rows, wide = amplitudes.shape
    deep = factors.shape[2]
    half = wide // 2
    dma = pltpu.SemaphoreType.DMA
    bf16 = jnp.bfloat16
    return pl.pallas_call(
        functools.partial(kernel, n),
        out_shape=jax.ShapeDtypeStruct((1, 3, pairs), jnp.float32),
        in_specs=[pl.BlockSpec(memory_space=pl.ANY)] * 2,
        out_specs=pl.BlockSpec(memory_space=pltpu.VMEM),
        scratch_shapes=[
            pltpu.VMEM((2, half, deep), bf16),
            pltpu.VMEM((2, half, deep), bf16),
            pltpu.VMEM((pairs, rows, wide), bf16),
            pltpu.VMEM((pairs, rows, half), bf16),
            pltpu.VMEM((2, pairs, rows, half), bf16),
            pltpu.VMEM((3, n, rows, half), bf16),
            pltpu.VMEM((3, n, rows, half), bf16),
            pltpu.VMEM((n, 8, 128), jnp.float32),
            pltpu.VMEM((2, n, 8, 128), jnp.float32),
            dma((2,)),
            dma((2, CHUNKS)),
            dma((2, CHUNKS)),
            dma((CHUNKS,)),
            dma((2,)),
            dma((3, n)),
            dma((3, n)),
            dma((2, n)),
            dma((2, n)),
        ],
        compiler_params=pltpu.CompilerParams(
            collective_id=0, has_side_effects=True, vmem_limit_bytes=61 * 2**20
        ),
    )(amplitudes, factors.reshape(2, half, deep))


def product_rows(left, right):
    return lax.dot_general(left, right, NT, preferred_element_type=jnp.float32).astype(jnp.bfloat16)


def gathered(n, amplitudes, factors):
    own = factors[0]
    near = lax.ppermute(factors, "blk", [(i, (i + n - 1) % n) for i in range(n)])[0]
    block = lax.all_gather(amplitudes, "blk", axis=1, tiled=True)
    cross = product_rows(own, near)
    tiles = jnp.stack([product_rows(own, own), cross, cross.T])
    total = jnp.einsum("pcd,kcd->kp", block, tiles, preferred_element_type=jnp.float32)
    return total[None]


def solution(mesh):
    n = mesh.shape["blk"]

    def body(amplitudes, factors):
        whole = amplitudes.shape[1] % 8 == 0 and n % 2 == 0 and mesh.shape["grp"] == 2
        return (fused if whole else gathered)(n, amplitudes, factors)

    return jax.shard_map(
        body,
        mesh=mesh,
        in_specs=(P("grp", "blk", None), P("blk", None, None)),
        out_specs=P("blk", None, "grp"),
        check_vma=False,
    )
```
